256 devices in a mesh: row: 32 (over y, z), col: 8 (over x, core).
Axes of the slice: x: 4, y: 4, z: 8, core: 2. Of those that a mesh axis runs over, the one named last changes fastest.
Arguments:
- hessian: bfloat16 [8, 3328, 26624], P(None, 'row', 'col'), may hold values from -0.026001572 to 5, as said below
- exponents: int32 [26624], P(('col', 'row')), may hold values from 0 to 1
- masks: int32 [26624, 256], P(('col', 'row')), may hold values 0 or 1
- weights: bfloat16 [26624, 256], P(('col', 'row')), may hold values from -12 to 12
Outputs:
- solution_field: float32 [26624, 256], P(('col', 'row'))
- residual: float32 [26624, 256], P(('col', 'row'))
The draws below stay inside these ranges and needn't reach their ends.
Inputs may be any that keep to these rules, and one draw needn't show every extreme that they name: `hessian`: read as an 26624 x 26624 matrix it is symmetric and positive definite.
All inputs are finite; a program needn't handle non-finite values. No bound on the sum of `masks` on one device may be relied on, other than what follows from the above.
Results may differ from the reference program's by a relative error of at most 0.014.
Values may be sent and summed in bfloat16 or wider, within the bound.
No kernel may reach another device: no remote copies, remote signals or barrier semaphores. Data moves between devices by JAX's collectives and lax.ppermute only.
A program may use at most 64 MiB of HBM per device.

```python
import math
import jax
import jax.numpy as jnp

N = 26624
K = 256
ITERS = 2
BLOCKS = 8
BLOCK_ROWS = 3328


def draw_hessian(key, part):
    key = jax.random.fold_in(key, 11)
    key_noise, key_diagonal, key_common = jax.random.split(key, 3)
    noise = jnp.clip(jax.random.normal(key_noise, (N, N), jnp.float32), -4.0, 4.0)
    diagonal = jax.random.uniform(key_diagonal, (N,), jnp.float32, 2.0, 4.0)
    strength = 3.0
    profile = jax.random.uniform(key_common, (N,), jnp.float32, 0.5, 1.5) * math.sqrt(strength / N)
    symmetric = (noise + noise.T) * (0.7 / math.sqrt(2.0 * N)) + profile[:, None] * profile[None, :]
    position = jnp.arange(N)
    symmetric = symmetric.at[position, position].set(diagonal)
    return symmetric.reshape(BLOCKS, BLOCK_ROWS, N).astype(jnp.bfloat16)


def draw_weights(key, part):
    key = jax.random.fold_in(key, 12)
    fraction = jnp.arange(N).astype(jnp.float32)[:, None] / N
    values = jnp.clip(jax.random.normal(key, (N, K), jnp.float32), -4.0, 4.0) + 0.8
    return (values * (1.0 + 1.5 * fraction)).astype(jnp.bfloat16)


def place_ends(result, key, least, largest):
    shape = result.shape
    place = [jax.random.randint(jax.random.fold_in(key, axis), (), 0, shape[axis]) for axis in range(len(shape))]
    result = result.at[tuple(place)].set(least)
    longest = shape.index(max(shape))
    place[longest] = (place[longest] + 1) % shape[longest]
    return result.at[tuple(place)].set(largest)


def setup_inputs(seed: int = 0) -> dict:
    streams_of = jax.random.split(jax.random.key(seed), 5)
    return {
        "hessian": draw_hessian(jax.random.fold_in(streams_of[4], 71), 0),
        "exponents": place_ends(jax.random.randint(streams_of[1], (N,), 0, 2), jax.random.fold_in(streams_of[1], 1), 0, 1).astype(jnp.int32),
        "masks": place_ends((jax.random.randint(streams_of[2], (N, K), 0, 5) < 2).astype(jnp.int32), jax.random.fold_in(streams_of[2], 1), 0, 1),
        "weights": draw_weights(jax.random.fold_in(streams_of[4], 71), 0),
    }


def reference(hessian, exponents, masks, weights):
    matrix = hessian.reshape(N, N)
    row_scale = jnp.exp2(-exponents.astype(jnp.float32))[:, None]
    kept = masks.astype(jnp.float32)
    dense = weights.astype(jnp.float32)

    def applied(vectors):
        rounded = (row_scale * vectors).astype(jnp.bfloat16)
        return kept * row_scale * jnp.dot(matrix, rounded, preferred_element_type=jnp.float32)

    solution_field = kept * dense
    residual = applied((1.0 - kept) * dense)
    direction = residual
    norm_now = jnp.sum(residual * residual, axis=0)
    for iteration in range(ITERS):
        image_now = applied(direction)
        step_size = norm_now / jnp.sum(direction * image_now, axis=0)
        solution_field = solution_field + step_size * direction
        residual = residual - step_size * image_now
        if iteration + 1 < ITERS:
            fresh = jnp.sum(residual * residual, axis=0)
            direction = residual + (fresh / norm_now) * direction
            norm_now = fresh
    return solution_field, residual
```

```python
import jax
import jax.numpy as jnp
from jax import lax
from jax.sharding import Mesh, PartitionSpec as P

Y, Z, X, CORE = 4, 8, 4, 2
BF16, F32 = jnp.bfloat16, jnp.float32


def spread(block, axes, size):
    return lax.all_to_all(jnp.broadcast_to(block[None], (size,) + block.shape), axes, 0, 0, tiled=True)


def gather_rows(block):
    along_z = spread(block, "z", Z)
    along_z = along_z.reshape(Z * block.shape[0], block.shape[1])
    whole = spread(along_z, "y", Y)
    return whole.reshape(Y * along_z.shape[0], block.shape[1])


def scatter_rows(partial_sum):
    core = lax.axis_index("core")
    split = partial_sum.reshape((X, CORE) + partial_sum.shape[1:])
    mine = lax.dynamic_index_in_dim(split, core, 1, keepdims=False)
    other = lax.dynamic_index_in_dim(split, 1 - core, 1, keepdims=False)
    half = mine + lax.ppermute(other, "core", [(0, 1), (1, 0)])
    return jnp.sum(lax.all_to_all(half, "x", 0, 0, tiled=True), axis=0)


def total_sums(sums):
    sums = jnp.sum(spread(sums, ("x", "core"), X * CORE), axis=0)
    return jnp.sum(spread(sums, ("y", "z"), Y * Z), axis=0)


def stack_sums(*rows):
    zero = jnp.zeros_like(rows[0])
    return jnp.stack(list(rows) + [zero] * (8 - len(rows)))


def column_sums(first, second):
    return jnp.sum(first * second, axis=0)


def on_device(hessian, exponents, masks, weights):
    row_scale = jnp.exp2(-exponents.astype(F32))[:, None]
    kept = masks.astype(F32)
    dense = weights.astype(F32)

    def applied(vectors):
        rounded = (row_scale * vectors).astype(BF16)
        partial_sum = jnp.einsum("cst,tk->csk", hessian, gather_rows(rounded), preferred_element_type=F32)
        return kept * row_scale * scatter_rows(partial_sum)

    solution_field = kept * dense
    first = applied((1.0 - kept) * dense)
    image = applied(first)
    sums = total_sums(
        stack_sums(column_sums(first, first), column_sums(first, image), column_sums(image, image))
    )
    norm, along, square = sums[0], sums[1], sums[2]
    step = norm / along
    residual = first - step * image
    fresh = norm - 2.0 * step * along + step * step * square
    direction = residual + fresh / norm * first
    solution_field = solution_field + step * first
    image = applied(direction)
    sums = total_sums(stack_sums(column_sums(direction, image)))
    step = fresh / sums[0]
    return (solution_field + step * direction, residual - step * image)


def solution(mesh):
    fine = Mesh(mesh.devices.reshape(Y, Z, X, CORE), ("y", "z", "x", "core"))
    owner = ("x", "core", "y", "z")
    in_specs = (
        P(None, ("y", "z"), ("x", "core")),
        P(owner),
        P(owner, None),
        P(owner, None),
    )
    out_specs = (P(owner, None), P(owner, None))
    return jax.shard_map(on_device, mesh=fine, in_specs=in_specs, out_specs=out_specs, check_vma=False)
```

```python
import jax
import jax.numpy as jnp
from jax import lax
from jax.sharding import Mesh, PartitionSpec as P

Y, Z, X, CORE = 4, 8, 4, 2
BF16, F32 = jnp.bfloat16, jnp.float32


def spread(block, axes, size):
    return lax.all_to_all(jnp.broadcast_to(block[None], (size,) + block.shape), axes, 0, 0, tiled=True)


def moved(block, axis, size, shift):
    return lax.ppermute(block, axis, [(i, (i + shift) % size) for i in range(size)])


def gather_rows(block):
    along_z = spread(block, "z", Z)
    along_z = along_z.reshape(Z * block.shape[0], block.shape[1])
    place = lax.axis_index("y")
    received = [moved(along_z, "y", Y, shift) for shift in (2, 1, 3)]
    whole = jnp.zeros((Y,) + along_z.shape, block.dtype)
    whole = lax.dynamic_update_index_in_dim(whole, along_z, place, 0)
    for shift, piece in zip((2, 1, 3), received):
        whole = lax.dynamic_update_index_in_dim(whole, piece, (place + Y - shift) % Y, 0)
    return whole.reshape(Y * along_z.shape[0], block.shape[1])


def scatter_rows(partial_sum):
    core = lax.axis_index("core")
    place = lax.axis_index("x")
    split = partial_sum.reshape((X, CORE) + partial_sum.shape[1:])
    mine = lax.dynamic_index_in_dim(split, core, 1, keepdims=False)
    other = lax.dynamic_index_in_dim(split, 1 - core, 1, keepdims=False)
    half = mine + lax.ppermute(other, "core", [(0, 1), (1, 0)])
    total = lax.dynamic_index_in_dim(half, place, 0, keepdims=False)
    for shift in (2, 1, 3):
        total = total + moved(lax.dynamic_index_in_dim(half, (place + shift) % X, 0, keepdims=False), "x", X, shift)
    return total


def total_sums(sums):
    sums = jnp.sum(spread(sums, ("x", "core"), X * CORE), axis=0)
    return jnp.sum(spread(sums, ("y", "z"), Y * Z), axis=0)


def stack_sums(*rows):
    zero = jnp.zeros_like(rows[0])
    return jnp.stack(list(rows) + [zero] * (8 - len(rows)))


def column_sums(first, second):
    return jnp.sum(first * second, axis=0)


def on_device(hessian, exponents, masks, weights):
    row_scale = jnp.exp2(-exponents.astype(F32))[:, None]
    kept = masks.astype(F32)
    dense = weights.astype(F32)

    def applied(vectors):
        rounded = (row_scale * vectors).astype(BF16)
        partial_sum = jnp.einsum("cst,tk->csk", hessian, gather_rows(rounded), preferred_element_type=F32)
        return kept * row_scale * scatter_rows(partial_sum)

    solution_field = kept * dense
    first = applied((1.0 - kept) * dense)
    image = applied(first)
    sums = total_sums(
        stack_sums(column_sums(first, first), column_sums(first, image), column_sums(image, image))
    )
    norm, along, square = sums[0], sums[1], sums[2]
    step = norm / along
    residual = first - step * image
    fresh = norm - 2.0 * step * along + step * step * square
    direction = residual + fresh / norm * first
    solution_field = solution_field + step * first
    image = applied(direction)
    sums = total_sums(stack_sums(column_sums(direction, image)))
    step = fresh / sums[0]
    return (solution_field + step * direction, residual - step * image)


def solution(mesh):
    fine = Mesh(mesh.devices.reshape(Y, Z, X, CORE), ("y", "z", "x", "core"))
    owner = ("x", "core", "y", "z")
    in_specs = (
        P(None, ("y", "z"), ("x", "core")),
        P(owner),
        P(owner, None),
        P(owner, None),
    )
    out_specs = (P(owner, None), P(owner, None))
    return jax.shard_map(on_device, mesh=fine, in_specs=in_specs, out_specs=out_specs, check_vma=False)
```

```python
import jax
import jax.numpy as jnp
from jax import lax
from jax.sharding import Mesh, PartitionSpec as P

Y, ZS, ZP, X, CORE = 4, 4, 2, 4, 2
BF16, F32 = jnp.bfloat16, jnp.float32
ROUNDING, ALLOWED = 8e-4, 8.5e-3


def spread(block, axes, size):
    return lax.all_to_all(jnp.broadcast_to(block[None], (size,) + block.shape), axes, 0, 0, tiled=True)


def gather_rows(block):
    strided = spread(block, "zs", ZS)
    whole = spread(strided, ("y", "zp"), Y * ZP)
    whole = whole.reshape((Y, ZP, ZS) + block.shape).transpose(0, 2, 1, 3, 4)
    return whole.reshape((Y * ZS * ZP,) + block.shape)


def moved(block, axis, size, shift):
    return lax.ppermute(block, axis, [(i, (i + shift) % size) for i in range(size)])


def scatter_rows(partial_sum):
    core = lax.axis_index("core")
    place = lax.axis_index("x")
    split = partial_sum.reshape((X, CORE) + partial_sum.shape[1:])
    mine = lax.dynamic_index_in_dim(split, core, 1, keepdims=False)
    other = lax.dynamic_index_in_dim(split, 1 - core, 1, keepdims=False)
    half = mine + lax.ppermute(other, "core", [(0, 1), (1, 0)])
    total = lax.dynamic_index_in_dim(half, place, 0, keepdims=False)
    for shift in (2, 1, 3):
        total = total + moved(lax.dynamic_index_in_dim(half, (place + shift) % X, 0, keepdims=False), "x", X, shift)
    return total


def total_sums(rows):
    sums = jnp.stack([jnp.sum(first * second, axis=0) for first, second in rows])
    sums = jnp.pad(sums, ((0, 8 - len(rows)), (0, 0)))
    sums = jnp.sum(spread(sums, ("x", "core"), X * CORE), axis=0)
    return jnp.sum(spread(sums, ("y", "zs", "zp"), Y * ZS * ZP), axis=0)


def on_device(hessian, exponents, masks, weights):
    row_scale = jnp.exp2(-exponents.astype(F32))[:, None]
    kept = masks.astype(F32)
    dense = weights.astype(F32)
    rows = exponents.shape[0]

    def product(gathered):
        gathered = gathered.reshape(-1, gathered.shape[-1])
        return jnp.einsum("cst,tk->csk", hessian, gathered, preferred_element_type=F32)

    def owned(partial_sum):
        return kept * row_scale * scatter_rows(partial_sum)

    start = lax.axis_index(("y", "zs", "zp")) * rows
    own_rows = lax.dynamic_index_in_dim(hessian, lax.axis_index(("x", "core")), 0, keepdims=False)
    on_diagonal = lax.broadcasted_iota(jnp.int32, own_rows.shape, 1) == start + lax.broadcasted_iota(
        jnp.int32, own_rows.shape, 0
    )
    diagonal = jnp.sum(jnp.where(on_diagonal, own_rows.astype(F32), 0.0), axis=1, keepdims=True)

    v0 = owned(product(gather_rows((row_scale * ((1.0 - kept) * dense)).astype(BF16))))

    scaled = row_scale * v0
    tail = jnp.stack([jnp.sum(diagonal * scaled * scaled, axis=0), jnp.sum(v0 * v0, axis=0)])
    tail = jnp.pad(tail, ((0, 6), (0, 0)))
    gathered = gather_rows(jnp.concatenate([scaled, tail]).astype(BF16))
    tails = jnp.sum(gathered[:, rows : rows + 2].astype(F32), axis=0)
    shift = jnp.where(tails[1] > 0.0, tails[0] / tails[1], 0.0)
    partial_0 = product(gathered[:, :rows])
    v1 = owned(partial_0)

    partial_1 = product(gather_rows((row_scale * (v1 - shift * v0)).astype(BF16)))
    v2 = owned(partial_1 + shift * partial_0)

    g00, g01, g11, g02, g12, g22, h1, h2 = total_sums(
        [(v0, v0), (v0, v1), (v1, v1), (v0, v2), (v1, v2), (v2, v2), (v0, shift * v0), (shift * v0, shift * v0)]
    )
    step_0 = g00 / g01
    residual = v0 - step_0 * v1
    fresh = g00 - 2.0 * step_0 * g01 + step_0 * step_0 * g11
    ahead = 1.0 + fresh / g00
    along = ahead * ahead * g01 - ahead * step_0 * (g02 + g11) + step_0 * step_0 * g12
    step_1 = fresh / along

    direction_sq = ahead * ahead * g00 - 2.0 * ahead * step_0 * g01 + step_0 * step_0 * g11
    left_sq = ahead * ahead * g00 - 2.0 * ahead * step_0 * h1 + step_0 * step_0 * h2
    with_image = ahead * g01 - step_0 * (g02 + ahead * g11) + step_0 * step_0 * g12
    image_sq = ahead * ahead * g11 - 2.0 * ahead * step_0 * g12 + step_0 * step_0 * g22
    last_sq = fresh - 2.0 * step_1 * with_image + step_1 * step_1 * image_sq
    spread_sq = left_sq + direction_sq + (jnp.sqrt(left_sq) + jnp.sqrt(direction_sq)) ** 2
    error_sq = ROUNDING**2 * jnp.sum(step_1 * step_1 * (g11 / g00) * spread_sq)
    close = error_sq < ALLOWED**2 * jnp.sum(last_sq)

    def short():
        direction = ahead * v0 - step_0 * v1
        image = ahead * v1 - step_0 * v2
        return (kept * dense + step_0 * v0 + step_1 * direction, residual - step_1 * image)

    def long():
        fresh = total_sums([(residual, residual)])[0]
        direction = residual + fresh / g00 * v0
        image = owned(product(gather_rows((row_scale * direction).astype(BF16))))
        step = fresh / total_sums([(direction, image)])[0]
        return (kept * dense + step_0 * v0 + step * direction, residual - step * image)

    return lax.cond(close, short, long)


def solution(mesh):
    fine = Mesh(mesh.devices.reshape(Y, ZS, ZP, X, CORE), ("y", "zs", "zp", "x", "core"))
    row = ("y", "zs", "zp")
    owner = ("x", "core") + row
    in_specs = (P(None, row, ("x", "core")), P(owner), P(owner, None), P(owner, None))
    out_specs = (P(owner, None), P(owner, None))
    return jax.shard_map(on_device, mesh=fine, in_specs=in_specs, out_specs=out_specs, check_vma=False)
```

```python
import jax
import jax.numpy as jnp
from jax import lax
from jax.sharding import Mesh, PartitionSpec as P

Y, ZS, ZP, X, CORE = 4, 4, 2, 4, 2
BF16, F32 = jnp.bfloat16, jnp.float32
ROUNDING, ALLOWED = 8e-4, 8.5e-3


def spread(block, axes, size):
    return lax.all_to_all(jnp.broadcast_to(block[None], (size,) + block.shape), axes, 0, 0, tiled=True)


def moved(block, axis, size, shift):
    return lax.ppermute(block, axis, [(i, (i + shift) % size) for i in range(size)])


def around(block, axis, size):
    place = lax.axis_index(axis)
    whole = jnp.zeros((size,) + block.shape, block.dtype)
    whole = lax.dynamic_update_index_in_dim(whole, block, place, 0)
    for shift in (2, 1, 3):
        whole = lax.dynamic_update_index_in_dim(whole, moved(block, axis, size, shift), (place + size - shift) % size, 0)
    return whole


def gather_rows(block):
    place, pair = lax.axis_index("y"), lax.axis_index("zp")
    strided = around(block, "zs", ZS)
    paired = lax.ppermute(strided, "zp", [(0, 1), (1, 0)])
    whole = jnp.zeros((Y, ZS, ZP) + block.shape, block.dtype)
    for piece, half in ((strided, pair), (paired, 1 - pair)):
        for shift in (0, 1, 3, 2):
            came = moved(piece, "y", Y, shift) if shift else piece
            at = ((place + Y - shift) % Y, 0, half, 0, 0)
            whole = lax.dynamic_update_slice(whole, came[None, :, None], at)
    return whole.reshape((Y * ZS * ZP,) + block.shape)


def scatter_rows(partial_sum):
    core = lax.axis_index("core")
    place = lax.axis_index("x")
    split = partial_sum.reshape((X, CORE) + partial_sum.shape[1:])
    mine = lax.dynamic_index_in_dim(split, core, 1, keepdims=False)
    other = lax.dynamic_index_in_dim(split, 1 - core, 1, keepdims=False)
    half = mine + lax.ppermute(other, "core", [(0, 1), (1, 0)])
    total = lax.dynamic_index_in_dim(half, place, 0, keepdims=False)
    for shift in (2, 1, 3):
        total = total + moved(lax.dynamic_index_in_dim(half, (place + shift) % X, 0, keepdims=False), "x", X, shift)
    return total


def total_sums(rows):
    sums = jnp.stack([jnp.sum(first * second, axis=0) for first, second in rows])
    sums = jnp.pad(sums, ((0, 8 - len(rows)), (0, 0)))
    sums = jnp.sum(spread(sums, ("x", "core"), X * CORE), axis=0)
    return jnp.sum(spread(sums, ("y", "zs", "zp"), Y * ZS * ZP), axis=0)


def on_device(hessian, exponents, masks, weights):
    row_scale = jnp.exp2(-exponents.astype(F32))[:, None]
    kept = masks.astype(F32)
    dense = weights.astype(F32)
    rows = exponents.shape[0]

    def product(gathered):
        gathered = gathered.reshape(-1, gathered.shape[-1])
        return jnp.einsum("cst,tk->csk", hessian, gathered, preferred_element_type=F32)

    def owned(partial_sum):
        return kept * row_scale * scatter_rows(partial_sum)

    start = lax.axis_index(("y", "zs", "zp")) * rows
    own_rows = lax.dynamic_index_in_dim(hessian, lax.axis_index(("x", "core")), 0, keepdims=False)
    on_diagonal = lax.broadcasted_iota(jnp.int32, own_rows.shape, 1) == start + lax.broadcasted_iota(
        jnp.int32, own_rows.shape, 0
    )
    diagonal = jnp.sum(jnp.where(on_diagonal, own_rows.astype(F32), 0.0), axis=1, keepdims=True)

    v0 = owned(product(gather_rows((row_scale * ((1.0 - kept) * dense)).astype(BF16))))

    scaled = row_scale * v0
    tail = jnp.stack([jnp.sum(diagonal * scaled * scaled, axis=0), jnp.sum(v0 * v0, axis=0)])
    tail = jnp.pad(tail, ((0, 6), (0, 0)))
    gathered = gather_rows(jnp.concatenate([scaled, tail]).astype(BF16))
    tails = jnp.sum(gathered[:, rows : rows + 2].astype(F32), axis=0)
    shift = jnp.where(tails[1] > 0.0, tails[0] / tails[1], 0.0)
    partial_0 = product(gathered[:, :rows])
    v1 = owned(partial_0)

    partial_1 = product(gather_rows((row_scale * (v1 - shift * v0)).astype(BF16)))
    v2 = owned(partial_1 + shift * partial_0)

    g00, g01, g11, g02, g12, g22, h1, h2 = total_sums(
        [(v0, v0), (v0, v1), (v1, v1), (v0, v2), (v1, v2), (v2, v2), (v0, shift * v0), (shift * v0, shift * v0)]
    )
    step_0 = g00 / g01
    residual = v0 - step_0 * v1
    fresh = g00 - 2.0 * step_0 * g01 + step_0 * step_0 * g11
    ahead = 1.0 + fresh / g00
    along = ahead * ahead * g01 - ahead * step_0 * (g02 + g11) + step_0 * step_0 * g12
    step_1 = fresh / along

    direction_sq = ahead * ahead * g00 - 2.0 * ahead * step_0 * g01 + step_0 * step_0 * g11
    left_sq = ahead * ahead * g00 - 2.0 * ahead * step_0 * h1 + step_0 * step_0 * h2
    with_image = ahead * g01 - step_0 * (g02 + ahead * g11) + step_0 * step_0 * g12
    image_sq = ahead * ahead * g11 - 2.0 * ahead * step_0 * g12 + step_0 * step_0 * g22
    last_sq = fresh - 2.0 * step_1 * with_image + step_1 * step_1 * image_sq
    spread_sq = left_sq + direction_sq + (jnp.sqrt(left_sq) + jnp.sqrt(direction_sq)) ** 2
    error_sq = ROUNDING**2 * jnp.sum(step_1 * step_1 * (g11 / g00) * spread_sq)
    close = error_sq < ALLOWED**2 * jnp.sum(last_sq)

    def short():
        direction = ahead * v0 - step_0 * v1
        image = ahead * v1 - step_0 * v2
        return (kept * dense + step_0 * v0 + step_1 * direction, residual - step_1 * image)

    def long():
        fresh = total_sums([(residual, residual)])[0]
        direction = residual + fresh / g00 * v0
        image = owned(product(gather_rows((row_scale * direction).astype(BF16))))
        step = fresh / total_sums([(direction, image)])[0]
        return (kept * dense + step_0 * v0 + step * direction, residual - step * image)

    return lax.cond(close, short, long)


def solution(mesh):
    fine = Mesh(mesh.devices.reshape(Y, ZS, ZP, X, CORE), ("y", "zs", "zp", "x", "core"))
    row = ("y", "zs", "zp")
    owner = ("x", "core") + row
    in_specs = (P(None, row, ("x", "core")), P(owner), P(owner, None), P(owner, None))
    out_specs = (P(owner, None), P(owner, None))
    return jax.shard_map(on_device, mesh=fine, in_specs=in_specs, out_specs=out_specs, check_vma=False)
```

```python
import jax
import jax.numpy as jnp
from jax import lax
from jax.sharding import Mesh, PartitionSpec as P

Y, ZS, ZP, X, CORE = 4, 4, 2, 4, 2
BF16, F32 = jnp.bfloat16, jnp.float32
ROUNDING, ALLOWED = 8e-4, 8.5e-3


def spread(block, axes, size):
    return lax.all_to_all(jnp.broadcast_to(block[None], (size,) + block.shape), axes, 0, 0, tiled=True)


def moved(block, axis, size, shift):
    return lax.ppermute(block, axis, [(i, (i + shift) % size) for i in range(size)])


def around(block, axis, size):
    place = lax.axis_index(axis)
    whole = jnp.zeros((size,) + block.shape, block.dtype)
    whole = lax.dynamic_update_index_in_dim(whole, block, place, 0)
    for shift in (2, 1, 3):
        whole = lax.dynamic_update_index_in_dim(whole, moved(block, axis, size, shift), (place + size - shift) % size, 0)
    return whole


def gather_rows(block):
    place, pair = lax.axis_index("y"), lax.axis_index("zp")
    swap = [(0, 1), (1, 0)]
    strided = around(block, "zs", ZS)
    mine = {shift: moved(strided, "y", Y, shift) for shift in (2, 1, 3)}
    paired = lax.ppermute(strided, "zp", swap)
    other = {shift: moved(paired, "y", Y, shift) for shift in (1, 3)}
    other[2] = lax.ppermute(mine[2], "zp", swap)
    mine[0], other[0] = strided, paired
    whole = jnp.zeros((Y, ZS, ZP) + block.shape, block.dtype)
    for pieces, half in ((mine, pair), (other, 1 - pair)):
        for shift, piece in pieces.items():
            at = ((place + Y - shift) % Y, 0, half, 0, 0)
            whole = lax.dynamic_update_slice(whole, piece[None, :, None], at)
    return whole.reshape((Y * ZS * ZP,) + block.shape)


def scatter_rows(partial_sum):
    core = lax.axis_index("core")
    place = lax.axis_index("x")
    split = partial_sum.reshape((X, CORE) + partial_sum.shape[1:])
    mine = lax.dynamic_index_in_dim(split, core, 1, keepdims=False)
    other = lax.dynamic_index_in_dim(split, 1 - core, 1, keepdims=False)
    half = mine + lax.ppermute(other, "core", [(0, 1), (1, 0)])
    total = lax.dynamic_index_in_dim(half, place, 0, keepdims=False)
    for shift in (2, 1, 3):
        total = total + moved(lax.dynamic_index_in_dim(half, (place + shift) % X, 0, keepdims=False), "x", X, shift)
    return total


def total_sums(rows):
    sums = jnp.stack([jnp.sum(first * second, axis=0) for first, second in rows])
    sums = jnp.pad(sums, ((0, 8 - len(rows)), (0, 0)))
    sums = jnp.sum(spread(sums, ("x", "core"), X * CORE), axis=0)
    return jnp.sum(spread(sums, ("y", "zs", "zp"), Y * ZS * ZP), axis=0)


def on_device(hessian, exponents, masks, weights):
    row_scale = jnp.exp2(-exponents.astype(F32))[:, None]
    kept = masks.astype(F32)
    dense = weights.astype(F32)
    rows = exponents.shape[0]

    def product(gathered):
        gathered = gathered.reshape(-1, gathered.shape[-1])
        return jnp.einsum("cst,tk->csk", hessian, gathered, preferred_element_type=F32)

    def owned(partial_sum):
        return kept * row_scale * scatter_rows(partial_sum)

    start = lax.axis_index(("y", "zs", "zp")) * rows
    own_rows = lax.dynamic_index_in_dim(hessian, lax.axis_index(("x", "core")), 0, keepdims=False)
    on_diagonal = lax.broadcasted_iota(jnp.int32, own_rows.shape, 1) == start + lax.broadcasted_iota(
        jnp.int32, own_rows.shape, 0
    )
    diagonal = jnp.sum(jnp.where(on_diagonal, own_rows.astype(F32), 0.0), axis=1, keepdims=True)

    v0 = owned(product(gather_rows((row_scale * ((1.0 - kept) * dense)).astype(BF16))))

    scaled = row_scale * v0
    tail = jnp.stack([jnp.sum(diagonal * scaled * scaled, axis=0), jnp.sum(v0 * v0, axis=0)])
    tail = jnp.pad(tail, ((0, 6), (0, 0)))
    gathered = gather_rows(jnp.concatenate([scaled, tail]).astype(BF16))
    tails = jnp.sum(gathered[:, rows : rows + 2].astype(F32), axis=0)
    shift = jnp.where(tails[1] > 0.0, tails[0] / tails[1], 0.0)
    partial_0 = product(gathered[:, :rows])
    v1 = owned(partial_0)

    partial_1 = product(gather_rows((row_scale * (v1 - shift * v0)).astype(BF16)))
    v2 = owned(partial_1 + shift * partial_0)

    g00, g01, g11, g02, g12, g22, h1, h2 = total_sums(
        [(v0, v0), (v0, v1), (v1, v1), (v0, v2), (v1, v2), (v2, v2), (v0, shift * v0), (shift * v0, shift * v0)]
    )
    step_0 = g00 / g01
    residual = v0 - step_0 * v1
    fresh = g00 - 2.0 * step_0 * g01 + step_0 * step_0 * g11
    ahead = 1.0 + fresh / g00
    along = ahead * ahead * g01 - ahead * step_0 * (g02 + g11) + step_0 * step_0 * g12
    step_1 = fresh / along

    direction_sq = ahead * ahead * g00 - 2.0 * ahead * step_0 * g01 + step_0 * step_0 * g11
    left_sq = ahead * ahead * g00 - 2.0 * ahead * step_0 * h1 + step_0 * step_0 * h2
    with_image = ahead * g01 - step_0 * (g02 + ahead * g11) + step_0 * step_0 * g12
    image_sq = ahead * ahead * g11 - 2.0 * ahead * step_0 * g12 + step_0 * step_0 * g22
    last_sq = fresh - 2.0 * step_1 * with_image + step_1 * step_1 * image_sq
    spread_sq = left_sq + direction_sq + (jnp.sqrt(left_sq) + jnp.sqrt(direction_sq)) ** 2
    error_sq = ROUNDING**2 * jnp.sum(step_1 * step_1 * (g11 / g00) * spread_sq)
    close = error_sq < ALLOWED**2 * jnp.sum(last_sq)

    def short():
        direction = ahead * v0 - step_0 * v1
        image = ahead * v1 - step_0 * v2
        return (kept * dense + step_0 * v0 + step_1 * direction, residual - step_1 * image)

    def long():
        fresh = total_sums([(residual, residual)])[0]
        direction = residual + fresh / g00 * v0
        image = owned(product(gather_rows((row_scale * direction).astype(BF16))))
        step = fresh / total_sums([(direction, image)])[0]
        return (kept * dense + step_0 * v0 + step * direction, residual - step * image)

    return lax.cond(close, short, long)


def solution(mesh):
    fine = Mesh(mesh.devices.reshape(Y, ZS, ZP, X, CORE), ("y", "zs", "zp", "x", "core"))
    row = ("y", "zs", "zp")
    owner = ("x", "core") + row
    in_specs = (P(None, row, ("x", "core")), P(owner), P(owner, None), P(owner, None))
    out_specs = (P(owner, None), P(owner, None))
    return jax.shard_map(on_device, mesh=fine, in_specs=in_specs, out_specs=out_specs, check_vma=False)
```

```python
import jax
import jax.numpy as jnp
from jax import lax
from jax.sharding import Mesh, PartitionSpec as P

Y, ZS, ZP, X, CORE = 4, 4, 2, 4, 2
BF16, F32 = jnp.bfloat16, jnp.float32
ROUNDING, ALLOWED = 8e-4, 8.5e-3


def spread(block, axes, size):
    return lax.all_to_all(jnp.broadcast_to(block[None], (size,) + block.shape), axes, 0, 0, tiled=True)


def moved(block, axis, size, shift):
    return lax.ppermute(block, axis, [(i, (i + shift) % size) for i in range(size)])


def around(block, axis, size):
    place = lax.axis_index(axis)
    whole = jnp.zeros((size,) + block.shape, block.dtype)
    whole = lax.dynamic_update_index_in_dim(whole, block, place, 0)
    for shift in (2, 1, 3):
        whole = lax.dynamic_update_index_in_dim(whole, moved(block, axis, size, shift), (place + size - shift) % size, 0)
    return whole


def gather_rows(block):
    place, pair = lax.axis_index("y"), lax.axis_index("zp")
    swap = [(0, 1), (1, 0)]
    strided = around(block, "zs", ZS)
    mine = {shift: moved(strided, "y", Y, shift) for shift in (2, 1, 3)}
    paired = lax.ppermute(strided, "zp", swap)
    other = {shift: moved(paired, "y", Y, shift) for shift in (1, 3)}
    other[2] = lax.ppermute(mine[2], "zp", swap)
    mine[0], other[0] = strided, paired
    whole = jnp.zeros((Y, ZS, ZP) + block.shape, block.dtype)
    for pieces, half in ((mine, pair), (other, 1 - pair)):
        for shift, piece in pieces.items():
            at = ((place + Y - shift) % Y, 0, half, 0, 0)
            whole = lax.dynamic_update_slice(whole, piece[None, :, None], at)
    return whole.reshape((Y * ZS * ZP,) + block.shape)


def scatter_rows(partial_sum):
    core = lax.axis_index("core")
    place = lax.axis_index("x")
    split = partial_sum.reshape((X, CORE) + partial_sum.shape[1:])
    mine = lax.dynamic_index_in_dim(split, core, 1, keepdims=False)
    other = lax.dynamic_index_in_dim(split, 1 - core, 1, keepdims=False)
    half = mine + lax.ppermute(other, "core", [(0, 1), (1, 0)])
    total = lax.dynamic_index_in_dim(half, place, 0, keepdims=False)
    for shift in (2, 1, 3):
        total = total + moved(lax.dynamic_index_in_dim(half, (place + shift) % X, 0, keepdims=False), "x", X, shift)
    return total


def gather_rows_seldom(block):
    strided = spread(block, "zs", ZS)
    whole = spread(strided, ("y", "zp"), Y * ZP)
    whole = whole.reshape((Y, ZP, ZS) + block.shape).transpose(0, 2, 1, 3, 4)
    return whole.reshape((Y * ZS * ZP,) + block.shape)


def scatter_rows_seldom(partial_sum):
    return jnp.sum(lax.all_to_all(partial_sum, ("x", "core"), 0, 0, tiled=True), axis=0)


def total_sums(rows):
    sums = jnp.stack([jnp.sum(first * second, axis=0) for first, second in rows])
    sums = jnp.pad(sums, ((0, 8 - len(rows)), (0, 0)))
    sums = jnp.sum(spread(sums, ("x", "core"), X * CORE), axis=0)
    return jnp.sum(spread(sums, ("y", "zs", "zp"), Y * ZS * ZP), axis=0)


def on_device(hessian, exponents, masks, weights):
    row_scale = jnp.exp2(-exponents.astype(F32))[:, None]
    kept = masks.astype(F32)
    dense = weights.astype(F32)
    rows = exponents.shape[0]

    def product(gathered):
        gathered = gathered.reshape(-1, gathered.shape[-1])
        return jnp.einsum("cst,tk->csk", hessian, gathered, preferred_element_type=F32)

    def owned(partial_sum):
        return kept * row_scale * scatter_rows(partial_sum)

    start = lax.axis_index(("y", "zs", "zp")) * rows
    own_rows = lax.dynamic_index_in_dim(hessian, lax.axis_index(("x", "core")), 0, keepdims=False)
    on_diagonal = lax.broadcasted_iota(jnp.int32, own_rows.shape, 1) == start + lax.broadcasted_iota(
        jnp.int32, own_rows.shape, 0
    )
    diagonal = jnp.sum(jnp.where(on_diagonal, own_rows.astype(F32), 0.0), axis=1, keepdims=True)

    v0 = owned(product(gather_rows((row_scale * ((1.0 - kept) * dense)).astype(BF16))))

    scaled = row_scale * v0
    tail = jnp.stack([jnp.sum(diagonal * scaled * scaled, axis=0), jnp.sum(v0 * v0, axis=0)])
    tail = jnp.pad(tail, ((0, 6), (0, 0)))
    gathered = gather_rows(jnp.concatenate([scaled, tail]).astype(BF16))
    tails = jnp.sum(gathered[:, rows : rows + 2].astype(F32), axis=0)
    shift = jnp.where(tails[1] > 0.0, tails[0] / tails[1], 0.0)
    partial_0 = product(gathered[:, :rows])
    v1 = owned(partial_0)

    partial_1 = product(gather_rows((row_scale * (v1 - shift * v0)).astype(BF16)))
    v2 = owned(partial_1 + shift * partial_0)

    g00, g01, g11, g02, g12, g22, h1, h2 = total_sums(
        [(v0, v0), (v0, v1), (v1, v1), (v0, v2), (v1, v2), (v2, v2), (v0, shift * v0), (shift * v0, shift * v0)]
    )
    step_0 = g00 / g01
    residual = v0 - step_0 * v1
    fresh = g00 - 2.0 * step_0 * g01 + step_0 * step_0 * g11
    ahead = 1.0 + fresh / g00
    along = ahead * ahead * g01 - ahead * step_0 * (g02 + g11) + step_0 * step_0 * g12
    step_1 = fresh / along

    direction_sq = ahead * ahead * g00 - 2.0 * ahead * step_0 * g01 + step_0 * step_0 * g11
    left_sq = ahead * ahead * g00 - 2.0 * ahead * step_0 * h1 + step_0 * step_0 * h2
    with_image = ahead * g01 - step_0 * (g02 + ahead * g11) + step_0 * step_0 * g12
    image_sq = ahead * ahead * g11 - 2.0 * ahead * step_0 * g12 + step_0 * step_0 * g22
    last_sq = fresh - 2.0 * step_1 * with_image + step_1 * step_1 * image_sq
    spread_sq = left_sq + direction_sq + (jnp.sqrt(left_sq) + jnp.sqrt(direction_sq)) ** 2
    error_sq = ROUNDING**2 * jnp.sum(step_1 * step_1 * (g11 / g00) * spread_sq)
    close = error_sq < ALLOWED**2 * jnp.sum(last_sq)

    def short():
        direction = ahead * v0 - step_0 * v1
        image = ahead * v1 - step_0 * v2
        return (kept * dense + step_0 * v0 + step_1 * direction, residual - step_1 * image)

    def long():
        fresh = total_sums([(residual, residual)])[0]
        direction = residual + fresh / g00 * v0
        partial_sum = product(gather_rows_seldom((row_scale * direction).astype(BF16)))
        image = kept * row_scale * scatter_rows_seldom(partial_sum)
        step = fresh / total_sums([(direction, image)])[0]
        return (kept * dense + step_0 * v0 + step * direction, residual - step * image)

    return lax.cond(close, short, long)


def solution(mesh):
    fine = Mesh(mesh.devices.reshape(Y, ZS, ZP, X, CORE), ("y", "zs", "zp", "x", "core"))
    row = ("y", "zs", "zp")
    owner = ("x", "core") + row
    in_specs = (P(None, row, ("x", "core")), P(owner), P(owner, None), P(owner, None))
    out_specs = (P(owner, None), P(owner, None))
    return jax.shard_map(on_device, mesh=fine, in_specs=in_specs, out_specs=out_specs, check_vma=False)
```

```python
import jax
import jax.numpy as jnp
from jax import lax
from jax.sharding import Mesh, PartitionSpec as P

Y, ZS, ZP, X, CORE = 4, 4, 2, 4, 2
BF16, F32 = jnp.bfloat16, jnp.float32
ROUNDING, ALLOWED = 8e-4, 8.5e-3


def spread(block, axes, size):
    return lax.all_to_all(jnp.broadcast_to(block[None], (size,) + block.shape), axes, 0, 0, tiled=True)


def moved(block, axis, size, shift):
    return lax.ppermute(block, axis, [(i, (i + shift) % size) for i in range(size)])


def around(block, axis, size):
    place = lax.axis_index(axis)
    whole = jnp.zeros((size,) + block.shape, block.dtype)
    whole = lax.dynamic_update_index_in_dim(whole, block, place, 0)
    for shift in (2, 1, 3):
        whole = lax.dynamic_update_index_in_dim(whole, moved(block, axis, size, shift), (place + size - shift) % size, 0)
    return whole


def gather_rows(block):
    place, pair = lax.axis_index("y"), lax.axis_index("zp")
    swap = [(0, 1), (1, 0)]
    strided = around(block, "zs", ZS)
    mine = {shift: moved(strided, "y", Y, shift) for shift in (2, 1, 3)}
    paired = lax.ppermute(strided, "zp", swap)
    other = {shift: moved(paired, "y", Y, shift) for shift in (1, 3)}
    other[2] = lax.ppermute(mine[2], "zp", swap)
    mine[0], other[0] = strided, paired
    whole = jnp.zeros((Y, ZS, ZP) + block.shape, block.dtype)
    for pieces, half in ((mine, pair), (other, 1 - pair)):
        for shift, piece in pieces.items():
            at = ((place + Y - shift) % Y, 0, half, 0, 0)
            whole = lax.dynamic_update_slice(whole, piece[None, :, None], at)
    return whole.reshape((Y * ZS * ZP,) + block.shape)


def scatter_rows(partial_sum):
    core = lax.axis_index("core")
    place = lax.axis_index("x")
    split = partial_sum.reshape((X, CORE) + partial_sum.shape[1:])
    mine = lax.dynamic_index_in_dim(split, core, 1, keepdims=False)
    other = lax.dynamic_index_in_dim(split, 1 - core, 1, keepdims=False)
    half = mine + lax.ppermute(other, "core", [(0, 1), (1, 0)])
    total = lax.dynamic_index_in_dim(half, place, 0, keepdims=False)
    for shift in (2, 1, 3):
        total = total + moved(lax.dynamic_index_in_dim(half, (place + shift) % X, 0, keepdims=False), "x", X, shift)
    return total


def gather_rows_seldom(block):
    strided = spread(block, "zs", ZS)
    whole = spread(strided, ("y", "zp"), Y * ZP)
    whole = whole.reshape((Y, ZP, ZS) + block.shape).transpose(0, 2, 1, 3, 4)
    return whole.reshape((Y * ZS * ZP,) + block.shape)


def scatter_rows_seldom(partial_sum):
    return jnp.sum(lax.all_to_all(partial_sum, ("x", "core"), 0, 0, tiled=True), axis=0)


def total_sums(rows):
    sums = jnp.stack([jnp.sum(first * second, axis=0) for first, second in rows])
    sums = jnp.pad(sums, ((0, 8 - len(rows)), (0, 0)))
    sums = jnp.sum(spread(sums, ("x", "core"), X * CORE), axis=0)
    return jnp.sum(spread(sums, ("y", "zs", "zp"), Y * ZS * ZP), axis=0)


def on_device(hessian, exponents, masks, weights):
    row_scale = jnp.exp2(-exponents.astype(F32))[:, None]
    kept = masks.astype(F32)
    dense = weights.astype(F32)
    rows = exponents.shape[0]

    def product(gathered):
        gathered = gathered.reshape(-1, gathered.shape[-1])
        return jnp.einsum("cst,tk->csk", hessian, gathered, preferred_element_type=F32)

    gain = kept * row_scale
    start = lax.axis_index(("y", "zs", "zp")) * rows
    block = lax.axis_index(("x", "core"))

    def turn(index, state):
        payload, found, last_partial, last_shift = state
        last = lax.dynamic_index_in_dim(found, jnp.maximum(index - 1, 0), 0, keepdims=False)

        gathered = gather_rows(payload)
        tails = jnp.sum(gathered[:, rows : rows + 2].astype(F32), axis=0)
        shift = jnp.where(tails[1] > 0.0, tails[0] / tails[1], last_shift)
        partial_sum = product(gathered[:, :rows]) + last_shift * last_partial
        vectors = gain * scatter_rows(partial_sum)

        own_rows = lax.dynamic_index_in_dim(hessian, block + jnp.minimum(index, 0), 0, keepdims=False)
        on_diagonal = lax.broadcasted_iota(jnp.int32, own_rows.shape, 1) == start + lax.broadcasted_iota(
            jnp.int32, own_rows.shape, 0
        )
        diagonal = jnp.sum(jnp.where(on_diagonal, own_rows.astype(F32), 0.0), axis=1, keepdims=True)

        scaled = row_scale * vectors
        tail = jnp.stack([jnp.sum(diagonal * scaled * scaled, axis=0), jnp.sum(vectors * vectors, axis=0)])
        tail = jnp.pad(jnp.where(index == 0, tail, 0.0), ((0, 6), (0, 0)))
        payload = jnp.concatenate([scaled - shift * (row_scale * last), tail]).astype(BF16)
        found = lax.dynamic_update_index_in_dim(found, vectors, index, 0)
        return payload, found, partial_sum, shift

    payload = jnp.pad((row_scale * ((1.0 - kept) * dense)).astype(BF16), ((0, 8), (0, 0)))
    found = jnp.zeros((3,) + dense.shape, F32)
    partial_sum = jnp.zeros(hessian.shape[:2] + dense.shape[1:], F32)
    _, (v0, v1, v2), _, shift = lax.fori_loop(0, 3, turn, (payload, found, partial_sum, partial_sum[0, 0]))

    g00, g01, g11, g02, g12, g22, h1, h2 = total_sums(
        [(v0, v0), (v0, v1), (v1, v1), (v0, v2), (v1, v2), (v2, v2), (v0, shift * v0), (shift * v0, shift * v0)]
    )
    step_0 = g00 / g01
    residual = v0 - step_0 * v1
    fresh = g00 - 2.0 * step_0 * g01 + step_0 * step_0 * g11
    ahead = 1.0 + fresh / g00
    along = ahead * ahead * g01 - ahead * step_0 * (g02 + g11) + step_0 * step_0 * g12
    step_1 = fresh / along

    direction_sq = ahead * ahead * g00 - 2.0 * ahead * step_0 * g01 + step_0 * step_0 * g11
    left_sq = ahead * ahead * g00 - 2.0 * ahead * step_0 * h1 + step_0 * step_0 * h2
    with_image = ahead * g01 - step_0 * (g02 + ahead * g11) + step_0 * step_0 * g12
    image_sq = ahead * ahead * g11 - 2.0 * ahead * step_0 * g12 + step_0 * step_0 * g22
    last_sq = fresh - 2.0 * step_1 * with_image + step_1 * step_1 * image_sq
    spread_sq = left_sq + direction_sq + (jnp.sqrt(left_sq) + jnp.sqrt(direction_sq)) ** 2
    error_sq = ROUNDING**2 * jnp.sum(step_1 * step_1 * (g11 / g00) * spread_sq)
    close = error_sq < ALLOWED**2 * jnp.sum(last_sq)

    def short():
        direction = ahead * v0 - step_0 * v1
        image = ahead * v1 - step_0 * v2
        return (kept * dense + step_0 * v0 + step_1 * direction, residual - step_1 * image)

    def long():
        fresh = total_sums([(residual, residual)])[0]
        direction = residual + fresh / g00 * v0
        partial_sum = product(gather_rows_seldom((row_scale * direction).astype(BF16)))
        image = kept * row_scale * scatter_rows_seldom(partial_sum)
        step = fresh / total_sums([(direction, image)])[0]
        return (kept * dense + step_0 * v0 + step * direction, residual - step * image)

    return lax.cond(close, short, long)


def solution(mesh):
    fine = Mesh(mesh.devices.reshape(Y, ZS, ZP, X, CORE), ("y", "zs", "zp", "x", "core"))
    row = ("y", "zs", "zp")
    owner = ("x", "core") + row
    in_specs = (P(None, row, ("x", "core")), P(owner), P(owner, None), P(owner, None))
    out_specs = (P(owner, None), P(owner, None))
    return jax.shard_map(on_device, mesh=fine, in_specs=in_specs, out_specs=out_specs, check_vma=False)
```

```python
import jax
import jax.numpy as jnp
from jax import lax
from jax.sharding import Mesh, PartitionSpec as P

Y, ZS, ZP, X, CORE = 4, 4, 2, 4, 2
BF16, F32 = jnp.bfloat16, jnp.float32
ROUNDING, ALLOWED = 8e-4, 8.5e-3


def spread(block, axes, size):
    return lax.all_to_all(jnp.broadcast_to(block[None], (size,) + block.shape), axes, 0, 0, tiled=True)


def moved(block, axis, size, shift):
    return lax.ppermute(block, axis, [(i, (i + shift) % size) for i in range(size)])


def around(block, axis, size):
    place = lax.axis_index(axis)
    whole = jnp.zeros((size,) + block.shape, block.dtype)
    whole = lax.dynamic_update_index_in_dim(whole, block, place, 0)
    for shift in (2, 1, 3):
        whole = lax.dynamic_update_index_in_dim(whole, moved(block, axis, size, shift), (place + size - shift) % size, 0)
    return whole


def gather_rows(block):
    place, pair = lax.axis_index("y"), lax.axis_index("zp")
    swap = [(0, 1), (1, 0)]
    strided = around(block, "zs", ZS)
    mine = {shift: moved(strided, "y", Y, shift) for shift in (2, 1, 3)}
    paired = lax.ppermute(strided, "zp", swap)
    other = {shift: moved(paired, "y", Y, shift) for shift in (1, 3)}
    other[2] = lax.ppermute(mine[2], "zp", swap)
    mine[0], other[0] = strided, paired
    whole = jnp.zeros((Y, ZS, ZP) + block.shape, block.dtype)
    for pieces, half in ((mine, pair), (other, 1 - pair)):
        for shift, piece in pieces.items():
            at = ((place + Y - shift) % Y, 0, half, 0, 0)
            whole = lax.dynamic_update_slice(whole, piece[None, :, None], at)
    return whole.reshape((Y * ZS * ZP,) + block.shape)


def scatter_rows(partial_sum):
    core, place = lax.axis_index("core"), lax.axis_index("x")
    split = partial_sum.reshape((X * CORE,) + partial_sum.shape[1:])

    def of_chip(shift):
        at = (place + shift) % X * CORE
        other = lax.dynamic_index_in_dim(split, at + 1 - core, 0, keepdims=False)
        return lax.dynamic_index_in_dim(split, at + core, 0, keepdims=False) + lax.ppermute(
            other, "core", [(0, 1), (1, 0)]
        )

    parts = [moved(of_chip(shift), "x", X, shift) for shift in (2, 1, 3)]
    return of_chip(0) + parts[0] + (parts[1] + parts[2])


def gather_rows_seldom(block):
    strided = spread(block, "zs", ZS)
    whole = spread(strided, ("y", "zp"), Y * ZP)
    whole = whole.reshape((Y, ZP, ZS) + block.shape).transpose(0, 2, 1, 3, 4)
    return whole.reshape((Y * ZS * ZP,) + block.shape)


def scatter_rows_seldom(partial_sum):
    return jnp.sum(lax.all_to_all(partial_sum, ("x", "core"), 0, 0, tiled=True), axis=0)


def total_sums(rows):
    sums = jnp.stack([jnp.sum(first * second, axis=0) for first, second in rows])
    sums = jnp.pad(sums, ((0, 8 - len(rows)), (0, 0)))
    sums = jnp.sum(spread(sums, ("x", "core"), X * CORE), axis=0)
    return jnp.sum(spread(sums, ("y", "zs", "zp"), Y * ZS * ZP), axis=0)


def on_device(hessian, exponents, masks, weights):
    row_scale = jnp.exp2(-exponents.astype(F32))[:, None]
    kept = masks.astype(F32)
    dense = weights.astype(F32)
    rows = exponents.shape[0]

    def product(gathered):
        gathered = gathered.reshape(-1, gathered.shape[-1])
        return jnp.einsum("cst,tk->csk", hessian, gathered, preferred_element_type=F32)

    gain = kept * row_scale
    start = lax.axis_index(("y", "zs", "zp")) * rows
    block = lax.axis_index(("x", "core"))

    def turn(index, state):
        payload, found, last_partial, last_shift = state
        last = lax.dynamic_index_in_dim(found, jnp.maximum(index - 1, 0), 0, keepdims=False)

        gathered = gather_rows(payload)
        tails = jnp.sum(gathered[:, rows : rows + 2].astype(F32), axis=0)
        shift = jnp.where(tails[1] > 0.0, tails[0] / tails[1], last_shift)
        partial_sum = product(gathered[:, :rows]) + last_shift * last_partial
        vectors = gain * scatter_rows(partial_sum)

        own_rows = lax.dynamic_index_in_dim(hessian, block + jnp.minimum(index, 0), 0, keepdims=False)
        on_diagonal = lax.broadcasted_iota(jnp.int32, own_rows.shape, 1) == start + lax.broadcasted_iota(
            jnp.int32, own_rows.shape, 0
        )
        diagonal = jnp.sum(jnp.where(on_diagonal, own_rows.astype(F32), 0.0), axis=1, keepdims=True)

        scaled = row_scale * vectors
        tail = jnp.stack([jnp.sum(diagonal * scaled * scaled, axis=0), jnp.sum(vectors * vectors, axis=0)])
        tail = jnp.pad(jnp.where(index == 0, tail, 0.0), ((0, 6), (0, 0)))
        payload = jnp.concatenate([scaled - shift * (row_scale * last), tail]).astype(BF16)
        found = lax.dynamic_update_index_in_dim(found, vectors, index, 0)
        return payload, found, partial_sum, shift

    payload = jnp.pad((row_scale * ((1.0 - kept) * dense)).astype(BF16), ((0, 8), (0, 0)))
    found = jnp.zeros((3,) + dense.shape, F32)
    partial_sum = jnp.zeros(hessian.shape[:2] + dense.shape[1:], F32)
    _, (v0, v1, v2), _, shift = lax.fori_loop(0, 3, turn, (payload, found, partial_sum, partial_sum[0, 0]))

    g00, g01, g11, g02, g12, g22, h1, h2 = total_sums(
        [(v0, v0), (v0, v1), (v1, v1), (v0, v2), (v1, v2), (v2, v2), (v0, shift * v0), (shift * v0, shift * v0)]
    )
    step_0 = g00 / g01
    residual = v0 - step_0 * v1
    fresh = g00 - 2.0 * step_0 * g01 + step_0 * step_0 * g11
    ahead = 1.0 + fresh / g00
    along = ahead * ahead * g01 - ahead * step_0 * (g02 + g11) + step_0 * step_0 * g12
    step_1 = fresh / along

    direction_sq = ahead * ahead * g00 - 2.0 * ahead * step_0 * g01 + step_0 * step_0 * g11
    left_sq = ahead * ahead * g00 - 2.0 * ahead * step_0 * h1 + step_0 * step_0 * h2
    with_image = ahead * g01 - step_0 * (g02 + ahead * g11) + step_0 * step_0 * g12
    image_sq = ahead * ahead * g11 - 2.0 * ahead * step_0 * g12 + step_0 * step_0 * g22
    last_sq = fresh - 2.0 * step_1 * with_image + step_1 * step_1 * image_sq
    spread_sq = left_sq + direction_sq + (jnp.sqrt(left_sq) + jnp.sqrt(direction_sq)) ** 2
    error_sq = ROUNDING**2 * jnp.sum(step_1 * step_1 * (g11 / g00) * spread_sq)
    close = error_sq < ALLOWED**2 * jnp.sum(last_sq)

    def short():
        direction = ahead * v0 - step_0 * v1
        image = ahead * v1 - step_0 * v2
        return (kept * dense + step_0 * v0 + step_1 * direction, residual - step_1 * image)

    def long():
        fresh = total_sums([(residual, residual)])[0]
        direction = residual + fresh / g00 * v0
        partial_sum = product(gather_rows_seldom((row_scale * direction).astype(BF16)))
        image = kept * row_scale * scatter_rows_seldom(partial_sum)
        step = fresh / total_sums([(direction, image)])[0]
        return (kept * dense + step_0 * v0 + step * direction, residual - step * image)

    return lax.cond(close, short, long)


def solution(mesh):
    fine = Mesh(mesh.devices.reshape(Y, ZS, ZP, X, CORE), ("y", "zs", "zp", "x", "core"))
    row = ("y", "zs", "zp")
    owner = ("x", "core") + row
    in_specs = (P(None, row, ("x", "core")), P(owner), P(owner, None), P(owner, None))
    out_specs = (P(owner, None), P(owner, None))
    return jax.shard_map(on_device, mesh=fine, in_specs=in_specs, out_specs=out_specs, check_vma=False)
```

```python
import jax
import jax.numpy as jnp
from jax import lax
from jax.sharding import Mesh, PartitionSpec as P

Y, ZS, ZP, X, CORE = 4, 4, 2, 4, 2
BF16, F32 = jnp.bfloat16, jnp.float32
ROUNDING, ALLOWED = 8e-4, 8.5e-3


def spread(block, axes, size):
    return lax.all_to_all(jnp.broadcast_to(block[None], (size,) + block.shape), axes, 0, 0, tiled=True)


def moved(block, axis, size, shift):
    return lax.ppermute(block, axis, [(i, (i + shift) % size) for i in range(size)])


def around(block, axis, size):
    place = lax.axis_index(axis)
    whole = jnp.zeros((size,) + block.shape, block.dtype)
    whole = lax.dynamic_update_index_in_dim(whole, block, place, 0)
    for shift in (2, 1, 3):
        whole = lax.dynamic_update_index_in_dim(whole, moved(block, axis, size, shift), (place + size - shift) % size, 0)
    return whole


def gather_rows(block):
    place, pair = lax.axis_index("y"), lax.axis_index("zp")
    swap = [(0, 1), (1, 0)]
    strided = around(block, "zs", ZS)
    mine = {shift: moved(strided, "y", Y, shift) for shift in (2, 1, 3)}
    paired = lax.ppermute(strided, "zp", swap)
    other = {shift: moved(paired, "y", Y, shift) for shift in (1, 3)}
    other[2] = lax.ppermute(mine[2], "zp", swap)
    mine[0], other[0] = strided, paired
    whole = jnp.zeros((Y, ZS, ZP) + block.shape, block.dtype)
    for pieces, half in ((mine, pair), (other, 1 - pair)):
        for shift, piece in pieces.items():
            at = ((place + Y - shift) % Y, 0, half, 0, 0)
            whole = lax.dynamic_update_slice(whole, piece[None, :, None], at)
    return whole.reshape((Y * ZS * ZP,) + block.shape)


def scatter_rows(partial_sum):
    core, place = lax.axis_index("core"), lax.axis_index("x")
    split = partial_sum.reshape((X * CORE,) + partial_sum.shape[1:])

    def of_chip(shift):
        at = (place + shift) % X * CORE
        other = lax.dynamic_index_in_dim(split, at + 1 - core, 0, keepdims=False)
        return lax.dynamic_index_in_dim(split, at + core, 0, keepdims=False) + lax.ppermute(
            other, "core", [(0, 1), (1, 0)]
        )

    parts = [moved(of_chip(shift), "x", X, shift) for shift in (2, 1, 3)]
    return of_chip(0) + parts[0] + (parts[1] + parts[2])


def gather_rows_seldom(block):
    strided = spread(block, "zs", ZS)
    whole = spread(strided, ("y", "zp"), Y * ZP)
    whole = whole.reshape((Y, ZP, ZS) + block.shape).transpose(0, 2, 1, 3, 4)
    return whole.reshape((Y * ZS * ZP,) + block.shape)


def scatter_rows_seldom(partial_sum):
    return jnp.sum(lax.all_to_all(partial_sum, ("x", "core"), 0, 0, tiled=True), axis=0)


def total_sums(rows):
    sums = jnp.stack([jnp.sum(first * second, axis=0) for first, second in rows])
    sums = jnp.pad(sums, ((0, 8 - len(rows)), (0, 0)))
    sums = sums + lax.ppermute(sums, "core", [(0, 1), (1, 0)])
    sums = jnp.sum(spread(sums, ("y", "x"), Y * X), axis=0)
    return jnp.sum(spread(sums, ("zs", "zp"), ZS * ZP), axis=0)


def on_device(hessian, exponents, masks, weights):
    row_scale = jnp.exp2(-exponents.astype(F32))[:, None]
    kept = masks.astype(F32)
    dense = weights.astype(F32)
    rows = exponents.shape[0]

    def product(gathered):
        gathered = gathered.reshape(-1, gathered.shape[-1])
        return jnp.einsum("cst,tk->csk", hessian, gathered, preferred_element_type=F32)

    gain = kept * row_scale
    start = lax.axis_index(("y", "zs", "zp")) * rows
    block = lax.axis_index(("x", "core"))

    def turn(index, state):
        payload, found, last_partial, last_shift = state
        last = lax.dynamic_index_in_dim(found, jnp.maximum(index - 1, 0), 0, keepdims=False)

        gathered = gather_rows(payload)
        tails = jnp.sum(gathered[:, rows : rows + 2].astype(F32), axis=0)
        shift = jnp.where(tails[1] > 0.0, tails[0] / tails[1], last_shift)
        partial_sum = product(gathered[:, :rows]) + last_shift * last_partial
        vectors = gain * scatter_rows(partial_sum)

        own_rows = lax.dynamic_index_in_dim(hessian, block + jnp.minimum(index, 0), 0, keepdims=False)
        on_diagonal = lax.broadcasted_iota(jnp.int32, own_rows.shape, 1) == start + lax.broadcasted_iota(
            jnp.int32, own_rows.shape, 0
        )
        diagonal = jnp.sum(jnp.where(on_diagonal, own_rows.astype(F32), 0.0), axis=1, keepdims=True)

        scaled = row_scale * vectors
        tail = jnp.stack([jnp.sum(diagonal * scaled * scaled, axis=0), jnp.sum(vectors * vectors, axis=0)])
        tail = jnp.pad(jnp.where(index == 0, tail, 0.0), ((0, 6), (0, 0)))
        payload = jnp.concatenate([scaled - shift * (row_scale * last), tail]).astype(BF16)
        found = lax.dynamic_update_index_in_dim(found, vectors, index, 0)
        return payload, found, partial_sum, shift

    payload = jnp.pad((row_scale * ((1.0 - kept) * dense)).astype(BF16), ((0, 8), (0, 0)))
    found = jnp.zeros((3,) + dense.shape, F32)
    partial_sum = jnp.zeros(hessian.shape[:2] + dense.shape[1:], F32)
    _, (v0, v1, v2), _, shift = lax.fori_loop(0, 3, turn, (payload, found, partial_sum, partial_sum[0, 0]))

    g00, g01, g11, g02, g12, g22, h1, h2 = total_sums(
        [(v0, v0), (v0, v1), (v1, v1), (v0, v2), (v1, v2), (v2, v2), (v0, shift * v0), (shift * v0, shift * v0)]
    )
    step_0 = g00 / g01
    residual = v0 - step_0 * v1
    fresh = g00 - 2.0 * step_0 * g01 + step_0 * step_0 * g11
    ahead = 1.0 + fresh / g00
    along = ahead * ahead * g01 - ahead * step_0 * (g02 + g11) + step_0 * step_0 * g12
    step_1 = fresh / along

    direction_sq = ahead * ahead * g00 - 2.0 * ahead * step_0 * g01 + step_0 * step_0 * g11
    left_sq = ahead * ahead * g00 - 2.0 * ahead * step_0 * h1 + step_0 * step_0 * h2
    with_image = ahead * g01 - step_0 * (g02 + ahead * g11) + step_0 * step_0 * g12
    image_sq = ahead * ahead * g11 - 2.0 * ahead * step_0 * g12 + step_0 * step_0 * g22
    last_sq = fresh - 2.0 * step_1 * with_image + step_1 * step_1 * image_sq
    spread_sq = left_sq + direction_sq + (jnp.sqrt(left_sq) + jnp.sqrt(direction_sq)) ** 2
    error_sq = ROUNDING**2 * jnp.sum(step_1 * step_1 * (g11 / g00) * spread_sq)
    close = error_sq < ALLOWED**2 * jnp.sum(last_sq)

    def short():
        direction = ahead * v0 - step_0 * v1
        image = ahead * v1 - step_0 * v2
        return (kept * dense + step_0 * v0 + step_1 * direction, residual - step_1 * image)

    def long():
        fresh = total_sums([(residual, residual)])[0]
        direction = residual + fresh / g00 * v0
        partial_sum = product(gather_rows_seldom((row_scale * direction).astype(BF16)))
        image = kept * row_scale * scatter_rows_seldom(partial_sum)
        step = fresh / total_sums([(direction, image)])[0]
        return (kept * dense + step_0 * v0 + step * direction, residual - step * image)

    return lax.cond(close, short, long)


def solution(mesh):
    fine = Mesh(mesh.devices.reshape(Y, ZS, ZP, X, CORE), ("y", "zs", "zp", "x", "core"))
    row = ("y", "zs", "zp")
    owner = ("x", "core") + row
    in_specs = (P(None, row, ("x", "core")), P(owner), P(owner, None), P(owner, None))
    out_specs = (P(owner, None), P(owner, None))
    return jax.shard_map(on_device, mesh=fine, in_specs=in_specs, out_specs=out_specs, check_vma=False)
```

```python
import jax
import jax.numpy as jnp
from jax import lax
from jax.sharding import Mesh, PartitionSpec as P

Y, ZS, ZP, X, CORE = 4, 4, 2, 4, 2
BF16, F32 = jnp.bfloat16, jnp.float32
ROUNDING, ALLOWED = 8e-4, 8.5e-3


def spread(block, axes, size):
    return lax.all_to_all(jnp.broadcast_to(block[None], (size,) + block.shape), axes, 0, 0, tiled=True)


def moved(block, axis, size, shift):
    return lax.ppermute(block, axis, [(i, (i + shift) % size) for i in range(size)])


def around(block, axis, size):
    place = lax.axis_index(axis)
    whole = jnp.zeros((size,) + block.shape, block.dtype)
    whole = lax.dynamic_update_index_in_dim(whole, block, place, 0)
    for shift in (2, 1, 3):
        whole = lax.dynamic_update_index_in_dim(whole, moved(block, axis, size, shift), (place + size - shift) % size, 0)
    return whole


def gather_rows(block):
    place, pair = lax.axis_index("y"), lax.axis_index("zp")
    swap = [(0, 1), (1, 0)]
    strided = around(block, "zs", ZS)
    mine = {shift: moved(strided, "y", Y, shift) for shift in (2, 1, 3)}
    paired = lax.ppermute(strided, "zp", swap)
    other = {shift: moved(paired, "y", Y, shift) for shift in (1, 3)}
    other[2] = lax.ppermute(mine[2], "zp", swap)
    mine[0], other[0] = strided, paired
    whole = jnp.zeros((Y, ZS, ZP) + block.shape, block.dtype)
    for pieces, half in ((mine, pair), (other, 1 - pair)):
        for shift, piece in pieces.items():
            at = ((place + Y - shift) % Y, 0, half, 0, 0)
            whole = lax.dynamic_update_slice(whole, piece[None, :, None], at)
    return whole.reshape((Y * ZS * ZP,) + block.shape)


def scatter_rows(partial_sum):
    core, place = lax.axis_index("core"), lax.axis_index("x")
    split = partial_sum.reshape((X * CORE,) + partial_sum.shape[1:])

    def of_chip(shift):
        at = (place + shift) % X * CORE
        other = lax.dynamic_index_in_dim(split, at + 1 - core, 0, keepdims=False)
        return lax.dynamic_index_in_dim(split, at + core, 0, keepdims=False) + lax.ppermute(
            other, "core", [(0, 1), (1, 0)]
        )

    parts = [moved(of_chip(shift), "x", X, shift) for shift in (2, 1, 3)]
    return of_chip(0) + parts[0] + (parts[1] + parts[2])


def gather_rows_seldom(block):
    strided = spread(block, "zs", ZS)
    whole = spread(strided, ("y", "zp"), Y * ZP)
    whole = whole.reshape((Y, ZP, ZS) + block.shape).transpose(0, 2, 1, 3, 4)
    return whole.reshape((Y * ZS * ZP,) + block.shape)


def scatter_rows_seldom(partial_sum):
    return jnp.sum(lax.all_to_all(partial_sum, ("x", "core"), 0, 0, tiled=True), axis=0)


def total_sums(rows):
    sums = jnp.stack([jnp.sum(first * second, axis=0) for first, second in rows])
    sums = jnp.pad(sums, ((0, 8 - len(rows)), (0, 0)))
    sums = sums + lax.ppermute(sums, "core", [(0, 1), (1, 0)])
    sums = jnp.sum(spread(sums, ("y", "x"), Y * X), axis=0)
    return jnp.sum(spread(sums, ("zs", "zp"), ZS * ZP), axis=0)


def on_device(hessian, exponents, masks, weights):
    row_scale = jnp.exp2(-exponents.astype(F32))[:, None]
    kept = masks.astype(F32)
    dense = weights.astype(F32)
    rows = exponents.shape[0]

    def product(gathered):
        gathered = gathered.reshape(-1, gathered.shape[-1])
        return jnp.einsum("cst,tk->csk", hessian, gathered, preferred_element_type=F32)

    gain = kept * row_scale
    start = lax.axis_index(("y", "zs", "zp")) * rows
    block = lax.axis_index(("x", "core"))

    def turn(index, state):
        payload, found, last_partial, last_shift = state
        last = lax.dynamic_index_in_dim(found, jnp.maximum(index - 1, 0), 0, keepdims=False)

        gathered = gather_rows(payload)
        tails = jnp.sum(gathered[:, rows : rows + 2].astype(F32), axis=0)
        shift = jnp.where(tails[1] > 0.0, tails[0] / tails[1], last_shift)
        partial_sum = product(gathered[:, :rows]) + last_shift * last_partial
        vectors = gain * scatter_rows(partial_sum)

        own_rows = lax.dynamic_index_in_dim(hessian, block + jnp.minimum(index, 0), 0, keepdims=False)
        on_diagonal = lax.broadcasted_iota(jnp.int32, own_rows.shape, 1) == start + lax.broadcasted_iota(
            jnp.int32, own_rows.shape, 0
        )
        diagonal = jnp.sum(jnp.where(on_diagonal, own_rows.astype(F32), 0.0), axis=1, keepdims=True)

        scaled = row_scale * vectors
        tail = jnp.stack([jnp.sum(diagonal * scaled * scaled, axis=0), jnp.sum(vectors * vectors, axis=0)])
        tail = jnp.pad(jnp.where(index == 0, tail, 0.0), ((0, 6), (0, 0)))
        payload = jnp.concatenate([scaled - shift * (row_scale * last), tail]).astype(BF16)
        found = lax.dynamic_update_index_in_dim(found, vectors, index, 0)
        return payload, found, partial_sum, shift

    payload = jnp.pad((row_scale * ((1.0 - kept) * dense)).astype(BF16), ((0, 8), (0, 0)))
    found = jnp.zeros((3,) + dense.shape, F32)
    partial_sum = jnp.zeros(hessian.shape[:2] + dense.shape[1:], F32)
    _, (v0, v1, v2), _, shift = lax.fori_loop(0, 3, turn, (payload, found, partial_sum, partial_sum[0, 0]))

    g00, g01, g11, g02, g12, g22, h1, h2 = total_sums(
        [(v0, v0), (v0, v1), (v1, v1), (v0, v2), (v1, v2), (v2, v2), (v0, shift * v0), (shift * v0, shift * v0)]
    )
    step_0 = g00 / g01
    residual = v0 - step_0 * v1
    fresh = g00 - 2.0 * step_0 * g01 + step_0 * step_0 * g11
    ahead = 1.0 + fresh / g00
    along = ahead * ahead * g01 - ahead * step_0 * (g02 + g11) + step_0 * step_0 * g12
    step_1 = fresh / along

    direction_sq = ahead * ahead * g00 - 2.0 * ahead * step_0 * g01 + step_0 * step_0 * g11
    left_sq = ahead * ahead * g00 - 2.0 * ahead * step_0 * h1 + step_0 * step_0 * h2
    with_image = ahead * g01 - step_0 * (g02 + ahead * g11) + step_0 * step_0 * g12
    image_sq = ahead * ahead * g11 - 2.0 * ahead * step_0 * g12 + step_0 * step_0 * g22
    last_sq = fresh - 2.0 * step_1 * with_image + step_1 * step_1 * image_sq
    spread_sq = left_sq + direction_sq + (jnp.sqrt(left_sq) + jnp.sqrt(direction_sq)) ** 2
    error_sq = ROUNDING**2 * jnp.sum(step_1 * step_1 * (g11 / g00) * spread_sq)
    close = error_sq < ALLOWED**2 * jnp.sum(last_sq)

    direction = ahead * v0 - step_0 * v1
    image = ahead * v1 - step_0 * v2
    short = (kept * dense + step_0 * v0 + step_1 * direction, residual - step_1 * image)

    def long():
        fresh = total_sums([(residual, residual)])[0]
        direction = residual + fresh / g00 * v0
        partial_sum = product(gather_rows_seldom((row_scale * direction).astype(BF16)))
        image = kept * row_scale * scatter_rows_seldom(partial_sum)
        step = fresh / total_sums([(direction, image)])[0]
        return (kept * dense + step_0 * v0 + step * direction, residual - step * image)

    return lax.cond(close, lambda: short, long)


def solution(mesh):
    fine = Mesh(mesh.devices.reshape(Y, ZS, ZP, X, CORE), ("y", "zs", "zp", "x", "core"))
    row = ("y", "zs", "zp")
    owner = ("x", "core") + row
    in_specs = (P(None, row, ("x", "core")), P(owner), P(owner, None), P(owner, None))
    out_specs = (P(owner, None), P(owner, None))
    return jax.shard_map(on_device, mesh=fine, in_specs=in_specs, out_specs=out_specs, check_vma=False)
```
